128 devices in a mesh: rows: 32 (over y, z, core), grp: 4 (over x).
Axes of the slice: x: 4, y: 4, z: 4, core: 2. Of those that a mesh axis runs over, the one named last changes fastest.
Arguments:
- table: bfloat16 [131072, 4096], P(('rows', 'grp')), may hold values from -24 to 24
- sketch: bfloat16 [4096, 256], replicated, may hold values from -0.09375 to 0.09375
- valid_counts: int32 [128], P(('rows', 'grp')), may hold values from 256 to 1024, as said below
Outputs:
- basis: float32 [131072, 256], P(('rows', 'grp'))
- coeffs: float32 [4096, 256], P(('rows', 'grp'))
The draws below stay inside these ranges and needn't reach their ends.
Inputs may be any that keep to these rules, and one draw needn't show every extreme that they name: `valid_counts`: some device uses all 1024 slots.
All inputs are finite; a program needn't handle non-finite values.
Results may differ from the reference program's by a relative error of at most 0.0039.
Values may be sent and summed in bfloat16 or wider, within the bound.
A program may use at most 64 MiB of HBM per device.

```python
import math
import jax
import jax.numpy as jnp
from jax import lax

D = 4096
K = 256
R_DEV = 1024
ROWS = 131072
N_ROWS = 32
N_GRP = 4


def draw_valid_counts(key, part):
    key = jax.random.fold_in(key, 7)
    first_key, second_key = jax.random.split(key)
    counts = jax.random.randint(first_key, (N_ROWS * N_GRP,), R_DEV // 4, R_DEV + 1)
    where_full = jax.random.randint(second_key, (), 0, N_ROWS * N_GRP)
    return counts.at[where_full].set(R_DEV).astype(jnp.int32)


def with_spikes(drawn, rng, source, target, shards_of, factor):
    owner, partner = [(jnp.arange(drawn.shape[axis_at]) // (drawn.shape[axis_at] // shards_of)).reshape([-1 if axis == axis_at else 1 for axis in range(drawn.ndim)]) for axis_at in (source, target)]
    chosen = jax.random.permutation(rng, shards_of)[partner]
    strong = (owner == chosen) | (owner == (partner + shards_of // 2) % shards_of)
    return jnp.where(strong, factor * drawn, drawn)


def shard_levels(key, extent, pieces, low, largest):
    gain, own = 1.0, jax.random.fold_in(key, 6)
    for axis_at, parts in pieces:
        draws = jnp.exp(jax.random.uniform(jax.random.fold_in(own, axis_at), (parts,), jnp.float32, low / len(pieces), largest / len(pieces)))
        gain = gain * jnp.repeat(draws, extent[axis_at] // parts).reshape([-1 if axis == axis_at else 1 for axis in range(len(extent))])
    return gain


def normal_values(key, shape, deviation, reach, cuts=(), held_as=jnp.bfloat16):
    drawn = jax.random.normal(key, shape, jnp.float32) * deviation
    if len(cuts) > 0:
        drawn = shard_levels(key, shape, cuts, -0.22, 0.18) * drawn
    return jnp.clip(drawn, min=-reach, max=reach).astype(held_as)


def bell_draw_with(rng, extent, deviation, most, cuts, heavy, kind=jnp.bfloat16):
    values = deviation * jax.random.normal(rng, extent, jnp.float32)
    if cuts:
        values = values * shard_levels(rng, extent, cuts, -0.22, 0.18)
    return jnp.clip(with_spikes(values, jax.random.fold_in(rng, 3), *heavy), -most, most).astype(kind)


def setup_inputs(seed: int = 0) -> dict:
    streams_of = jax.random.split(jax.random.key(seed), 4)
    table = bell_draw_with(streams_of[0], (ROWS, D), 1.0, 24.0, ((0, 128),), (0, 1, 128, 5.5))
    sketch = normal_values(streams_of[1], (D, K), D ** -0.5, 0.09375)
    valid_counts = draw_valid_counts(jax.random.fold_in(streams_of[3], 71), 0)
    return dict(table=table, sketch=sketch, valid_counts=valid_counts)


def orthonormal(first):
    gram = jnp.dot(first.T.astype(jnp.float32), first.astype(jnp.float32), precision=lax.Precision.HIGHEST, preferred_element_type=jnp.float32)
    lower = jnp.linalg.cholesky(gram)
    return lax.linalg.triangular_solve(lower, first, left_side=False, lower=True, transpose_a=True)

def reference(table, sketch, valid_counts):
    slot = jnp.arange(ROWS, dtype=jnp.int32)
    owner = slot // R_DEV
    used = slot % R_DEV < valid_counts[owner]
    masked = jnp.where(used[:, None], table, jnp.zeros_like(table))
    first = jnp.dot(masked.astype(jnp.float32), sketch.astype(jnp.float32), preferred_element_type=jnp.float32)
    ortho_one = orthonormal(first).astype(jnp.bfloat16)
    project = jnp.dot(masked.T.astype(jnp.float32), ortho_one.astype(jnp.float32), preferred_element_type=jnp.float32).astype(jnp.bfloat16)
    second = jnp.dot(masked.astype(jnp.float32), project.astype(jnp.float32), preferred_element_type=jnp.float32)
    ortho_two = orthonormal(second)
    basis = ortho_two * math.sqrt(ROWS)
    coeffs = jnp.dot(masked.T.astype(jnp.float32), ortho_two.astype(jnp.bfloat16).astype(jnp.float32), preferred_element_type=jnp.float32)
    return (basis, coeffs)
```

```python
import functools
import math

import jax
import jax.numpy as jnp
from jax import lax
from jax.experimental import pallas as pl
from jax.experimental.pallas import tpu as pltpu
from jax.sharding import PartitionSpec as P

MESH = pl.DeviceIdType.MESH
HIGHEST = lax.Precision.HIGHEST
f32 = jnp.float32
bf16 = jnp.bfloat16

SLOTS = 1024
WIDTH = 4096
COLS = 256
CHIPS = 64
BLOCK = 32
PANEL = 64
GROUP = 16
CHUNKS = 2
VMEM_BYTES = 48 * 1024 * 1024


def dot_t(a, b, precision=None):
    return lax.dot_general(
        a, b, (((0,), (0,)), ((), ())), precision=precision, preferred_element_type=f32
    )


def dot_nt(a, b, precision=None):
    return lax.dot_general(
        a, b, (((1,), (1,)), ((), ())), precision=precision, preferred_element_type=f32
    )


def inverse_of_factor(gram, between=None):
    n = gram.shape[0]
    lane = lax.broadcasted_iota(jnp.int32, (PANEL, n), 1)
    sub = lax.broadcasted_iota(jnp.int32, (PANEL, n), 0)
    sub_narrow = lax.broadcasted_iota(jnp.int32, (PANEL, 128), 0)
    rest = gram
    rows = []
    for start in range(0, n, PANEL):
        end = start + PANEL
        if between is not None and end == n:
            between()
        panel = rest[0:PANEL, :]
        for low in range(0, PANEL, GROUP):
            spread = [
                jnp.broadcast_to(panel[:, start + t : start + t + 1], (PANEL, 128))
                for t in range(low, low + GROUP)
            ]
            for k in range(GROUP):
                t = low + k
                j = start + t
                inv = 1.0 / spread[k][t : t + 1, :]
                factor = jnp.where(sub_narrow > t, spread[k], 0.0)
                for m in range(k + 1, GROUP):
                    spread[m] = spread[m] - factor * (spread[m][t : t + 1, :] * inv)
                pivot = jnp.where(lane[0:1] == j, 1.0, panel[t : t + 1, :])
                pivot = pivot * jnp.concatenate([inv, inv], axis=1)
                kept = jnp.where((sub > t) & (lane == j), 0.0, panel)
                panel = kept - jnp.concatenate([factor, factor], axis=1) * pivot
        diagonal = lane == sub + start
        d = jnp.sum(jnp.where(diagonal, panel, 0.0), axis=1, keepdims=True)
        right = jnp.where(diagonal, 1.0, jnp.where(lane < sub + start, panel, 0.0))
        rows.append(right * lax.rsqrt(d))
        if end < n:
            left = jnp.where(lane >= end, panel, 0.0)
            update = dot_t(left * (1.0 / d), left + right, HIGHEST)
            lane_rest = lax.broadcasted_iota(jnp.int32, (n - end, n), 1)
            inside = (lane_rest >= start) & (lane_rest < end)
            rest = jnp.where(inside, 0.0, rest[PANEL:, :]) - update[end:, :]
    return jnp.concatenate(rows, axis=0)


def range_kernel(
    table_hbm, sketch, counts,
    ortho_out, coeffs_out,
    table, first, rounded, zfull, total,
    zpart, zcore, zsend, zrecv, zblock,
    wpart, wcore, wsend, wrecv,
    gsend, gcore, gsum, grecv, gown, gfull,
    load_sem, core_ss, core_rs, rs_ss, rs_rs, ag_ss, ag_rs, fw_ss, fw_rs,
    g_ss, g_rs, gs_ss, gs_rs, gg_ss, gg_rs, gx_ss, gx_rs,
):
    rows = lax.axis_index("rows")
    x = lax.axis_index("grp")
    core = lax.rem(rows, 2)
    z = lax.rem(rows // 2, 4)
    y = rows // 8
    chip = (y * 4 + z) * 4 + x
    sib = {"rows": rows + 1 - 2 * core}

    def peer(i):
        py = lax.rem(y + i // 16, 4)
        pz = lax.rem(z + lax.rem(i // 4, 4), 4)
        px = lax.rem(x + lax.rem(i, 4), 4)
        return py, pz, px, ((py * 4 + pz) * 2 + core, px)

    def remote(src, dst, ss, rs, device):
        return pltpu.make_async_remote_copy(
            src_ref=src, dst_ref=dst, send_sem=ss, recv_sem=rs,
            device_id=device, device_id_type=MESH,
        )

    def whole(ref, ss, rs):
        return remote(ref, ref, ss, rs, sib)

    loads = []
    for k in range(4):
        r = pl.ds(k * 256, 256)
        loads.append(pltpu.make_async_copy(table_hbm.at[r], table.at[r], load_sem.at[k]))
    for copy in loads:
        copy.start()

    barrier = pltpu.get_barrier_semaphore()

    @pl.loop(1, CHIPS)
    def _(i):
        pl.semaphore_signal(barrier, inc=1, device_id=peer(i)[3], device_id_type=MESH)

    pl.semaphore_signal(barrier, inc=1, device_id=sib, device_id_type=MESH)

    count = counts[0]
    for k in range(4):
        r = pl.ds(k * 256, 256)
        loads[k].wait()
        value = jnp.dot(table[r, :], sketch[...], preferred_element_type=f32)
        used = lax.broadcasted_iota(jnp.int32, (256, COLS), 0) + k * 256 < count
        value = jnp.where(used, value, 0.0)
        first[r, :] = value

    pl.semaphore_wait(barrier, CHIPS)

    zblk = BLOCK // CHUNKS
    sums = [
        (zpart.at[q], zcore.at[q], zsend.at[q], zrecv.at[q], q * (WIDTH // CHUNKS), zblk)
        for q in range(CHUNKS)
    ]
    sums.append((wpart, wcore, wsend, wrecv, 0, BLOCK))

    def line(k, j, sign=1):
        return lax.rem(y + 4 + sign * j, 4) * 4 + lax.rem(z + 4 + sign * ((k - j) % 4), 4)

    def member(i, k):
        j = i // 4
        py = lax.rem(y + j, 4)
        pz = lax.rem(z + lax.rem(k + 4 - j, 4), 4)
        px = lax.rem(x + lax.rem(i, 4), 4)
        return ((py * 4 + pz) * 2 + core, px), px

    def core_copy(q, k):
        part, core_recv = sums[q][:2]
        return remote(
            part.at[k, :, 1 - core], core_recv.at[k], core_ss.at[q, k], core_rs.at[q, k], sib
        )

    def produce(q, k):
        part, _, _, _, base, block = sums[q]
        for j in range(4):
            cols = pl.ds(pl.multiple_of(base + line(k, j) * (8 * block), 8 * block), 8 * block)
            value = dot_t(table[:, cols], rounded[...])
            part[k, j] = value.astype(part.dtype).reshape(2, 4, block, COLS)
        core_copy(q, k).start()

    def spread(q, k):
        part, core_recv, send, recv = sums[q][:4]
        core_copy(q, k).wait_recv()
        mine = part[k, :, core].astype(f32)
        send[k] = (mine + core_recv[k].astype(f32)).astype(send.dtype)

        @pl.loop(1 if k == 0 else 0, 16)
        def _(i):
            device, px = member(i, k)
            remote(
                send.at[k, i // 4, px], recv.at[k * 16 + i], rs_ss.at[q], rs_rs.at[q, k], device
            ).start()

    def reduce_end(q):
        send, recv = sums[q][2:4]
        acc = send[0, 0, x].astype(f32)
        for k in range(4):
            low = k * 16 + (1 if k == 0 else 0)
            n = k * 16 + 16 - low
            whole(recv.at[pl.ds(low, n)], rs_ss.at[q], rs_rs.at[q, k]).wait_recv()
            acc = acc + jnp.sum(recv[pl.ds(low, n)].astype(f32), axis=0)
        return acc

    mine = core * 24
    owner = (chip >= mine) & (chip < mine + 24)

    def gram_exchange(u):
        return remote(
            gsend.at[u, pl.ds(24 - mine, 24)], gcore.at[u], gx_ss.at[u], gx_rs.at[u], sib
        )

    def gram_start(u):
        gram = dot_t(first[...], first[...], HIGHEST)
        gsend[u, pl.ds(0, 16)] = gram[:128, :128].reshape(16, 8, 128)
        gsend[u, pl.ds(16, 16)] = gram[128:, :128].reshape(16, 8, 128)
        gsend[u, pl.ds(32, 16)] = gram[128:, 128:].reshape(16, 8, 128)
        gram_exchange(u).start()

    def gram_send(u):
        gram_exchange(u).wait()
        gsum[u] = gsend[u, pl.ds(mine, 24)] + gcore[u]

        @pl.loop(0, 24)
        def _(k):
            t = mine + k
            device = (((t // 16) * 4 + lax.rem(t // 4, 4)) * 2 + core, lax.rem(t, 4))

            @pl.when(t != chip)
            def _():
                remote(
                    gsum.at[u, k], grecv.at[u, chip], g_ss.at[u], g_rs.at[u], device
                ).start()

    def tiles(u, n, ss, rs):
        return whole(grecv.at[u, pl.ds(0, n)], ss.at[u], rs.at[u])

    def gram_mid(u):
        @pl.when(owner)
        def _():
            grecv[u, chip] = gsum[u, chip - mine]
            tiles(u, 63, g_ss, g_rs).wait_recv()
            tile = jnp.sum(grecv[u], axis=0)
            gown[u] = tile
            gfull[u, chip] = tile

            @pl.loop(1, CHIPS)
            def _(i):
                remote(
                    gown.at[u], gfull.at[u, chip], gg_ss.at[u], gg_rs.at[u], peer(i)[3]
                ).start()

    def gram_end(u):
        @pl.when(owner)
        def _():
            tiles(u, 23, g_ss, gg_rs).wait()
            tiles(u, 63, gg_ss, gg_rs).wait_send()

        @pl.when(jnp.logical_not(owner))
        def _():
            tiles(u, 24, g_ss, gg_rs).wait()

        half = gfull.at[u, pl.ds(mine, 24)]
        back = remote(half, half, gs_ss.at[u], gs_rs.at[u], sib)
        back.start()
        back.wait()
        blocks = [gfull[u, pl.ds(16 * b, 16)].reshape(128, 128) for b in range(3)]
        top = jnp.concatenate([blocks[0], blocks[1].T], axis=1)
        return jnp.concatenate([top, jnp.concatenate(blocks[1:], axis=1)], axis=0)

    def gather_start(q):
        value = reduce_end(q).astype(bf16)
        zblock[q] = value
        home = zfull.at[q, y * 4 + z, core, x]
        home[...] = value
        for k in range(4):

            @pl.loop(1 if k == 0 else 0, 16)
            def _(i):
                device = member(i, k)[0]
                remote(zblock.at[q], home, ag_ss.at[q], ag_rs.at[q, k], device).start()

    def fw_copies(q, k):
        return [
            whole(zfull.at[q, line(k, j, -1), core], fw_ss.at[q, k], fw_rs.at[q, k])
            for j in range(4)
        ]

    def forward(q, k):
        n = 15 if k == 0 else 16
        whole(zfull.at[q, pl.ds(0, n), 0, 0], ag_ss.at[q], ag_rs.at[q, k]).wait_recv()
        for copy in fw_copies(q, k):
            copy.start()

    def multiply(q, k):
        whole(zfull.at[q, pl.ds(0, 4), 0], fw_ss.at[q, k], fw_rs.at[q, k]).wait_recv()
        value = None
        for j in range(4):
            at = line(k, j, -1)
            cols = pl.ds(
                pl.multiple_of(q * (WIDTH // CHUNKS) + at * (8 * zblk), 8 * zblk), 8 * zblk
            )
            piece = zfull[q, at].reshape(8 * zblk, COLS)
            term = jnp.dot(table[:, cols], piece, preferred_element_type=f32)
            value = term if value is None else value + term
        if (q, k) == (0, 0):
            total[...] = value
        else:
            total[...] += value

    steps = [(q, k) for q in range(CHUNKS) for k in range(4)]

    gram_start(0)
    gram_send(0)
    gram_mid(0)
    inverse = inverse_of_factor(gram_end(0))
    rounded[...] = dot_nt(first[...], inverse, HIGHEST).astype(bf16)
    produce(*steps[0])
    for n in range(1, len(steps)):
        produce(*steps[n])
        spread(*steps[n - 1])
    spread(*steps[-1])
    for q in range(CHUNKS):
        gather_start(q)
    forward(*steps[0])
    for n in range(1, len(steps)):
        forward(*steps[n])
        multiply(*steps[n - 1])
    multiply(*steps[-1])

    value = total[...]
    used = lax.broadcasted_iota(jnp.int32, (SLOTS, COLS), 0) < count
    first[...] = jnp.where(used, value, 0.0)
    gram_start(1)

    every = zfull[...].reshape(WIDTH, COLS)
    near = dot_t(every, every)
    gram_send(1)
    near = jnp.dot(near, near, precision=HIGHEST, preferred_element_type=f32)
    guess = inverse_of_factor(near, lambda: gram_mid(1))
    broken = jnp.sum(jnp.where(guess - guess == 0.0, 0.0, 1.0), keepdims=True)
    r = lax.broadcasted_iota(jnp.int32, (COLS, COLS), 0)
    c = lax.broadcasted_iota(jnp.int32, (COLS, COLS), 1)
    guess = jnp.where(broken > 0.0, jnp.where(r == c, 1.0, 0.0), guess)
    value = dot_nt(first[...], guess, HIGHEST)
    first[...] = value
    rounded[...] = value.astype(bf16)

    w = CHUNKS
    produce(w, 0)
    for k in range(1, 4):
        produce(w, k)
        spread(w, k - 1)
    spread(w, 3)

    gram = jnp.dot(guess, gram_end(1), precision=HIGHEST, preferred_element_type=f32)
    inverse = inverse_of_factor(dot_nt(gram, guess, HIGHEST))
    total[...] = dot_nt(first[...], inverse, HIGHEST)
    out = pltpu.make_async_copy(total, ortho_out, load_sem.at[5])
    out.start()
    coeffs_out[...] = dot_nt(reduce_end(w), inverse, HIGHEST)

    out.wait()
    for q in range(CHUNKS + 1):
        for k in range(4):
            core_copy(q, k).wait_send()
        recv = sums[q][3]
        whole(recv.at[pl.ds(1, 63)], rs_ss.at[q], rs_rs.at[q, 0]).wait_send()
    for q in range(CHUNKS):
        for k in range(4):
            n = 15 if k == 0 else 16
            whole(zfull.at[q, pl.ds(0, n), 0, 0], ag_ss.at[q], ag_rs.at[q, k]).wait_send()
            whole(zfull.at[q, pl.ds(0, 4), 0], fw_ss.at[q, k], fw_rs.at[q, k]).wait_send()


def on_device(table, sketch, valid_counts):
    dma = pltpu.SemaphoreType.DMA
    vmem = pltpu.VMEM
    ortho, coeffs = pl.pallas_call(
        range_kernel,
        out_shape=(
            jax.ShapeDtypeStruct((SLOTS, COLS), f32),
            jax.ShapeDtypeStruct((BLOCK, COLS), f32),
        ),
        in_specs=[
            pl.BlockSpec(memory_space=pl.ANY),
            pl.BlockSpec(memory_space=pltpu.VMEM),
            pl.BlockSpec(memory_space=pltpu.SMEM),
        ],
        out_specs=(
            pl.BlockSpec(memory_space=pl.ANY),
            pl.BlockSpec(memory_space=pltpu.VMEM),
        ),
        scratch_shapes=[
            vmem((SLOTS, WIDTH), bf16),
            vmem((SLOTS, COLS), f32),
            vmem((SLOTS, COLS), bf16),
            vmem((CHUNKS, 16, 2, 4, BLOCK // CHUNKS, COLS), bf16),
            vmem((SLOTS, COLS), f32),
            vmem((CHUNKS, 4, 4, 2, 4, BLOCK // CHUNKS, COLS), bf16),
            vmem((CHUNKS, 4, 4, 4, BLOCK // CHUNKS, COLS), bf16),
            vmem((CHUNKS, 4, 4, 4, BLOCK // CHUNKS, COLS), bf16),
            vmem((CHUNKS, CHIPS, BLOCK // CHUNKS, COLS), bf16),
            vmem((CHUNKS, BLOCK // CHUNKS, COLS), bf16),
            vmem((4, 4, 2, 4, BLOCK, COLS), bf16),
            vmem((4, 4, 4, BLOCK, COLS), bf16),
            vmem((4, 4, 4, BLOCK, COLS), bf16),
            vmem((CHIPS, BLOCK, COLS), bf16),
            vmem((2, 48, 8, 128), f32),
            vmem((2, 24, 8, 128), f32),
            vmem((2, 24, 8, 128), f32),
            vmem((2, CHIPS, 8, 128), f32),
            vmem((2, 8, 128), f32),
            vmem((2, 48, 8, 128), f32),
            dma((6,)),
            dma((3, 4)),
            dma((3, 4)),
            dma((3,)),
            dma((3, 4)),
            dma((2,)),
            dma((2, 4)),
            dma((2, 4)),
            dma((2, 4)),
            dma((2,)),
            dma((2,)),
            dma((2,)),
            dma((2,)),
            dma((2,)),
            dma((2,)),
            dma((2,)),
            dma((2,)),
        ],
        compiler_params=pltpu.CompilerParams(
            collective_id=0, has_side_effects=True, vmem_limit_bytes=VMEM_BYTES
        ),
        name="range",
    )(table, sketch, valid_counts)
    return ortho * math.sqrt(SLOTS * 128), coeffs


def solution(mesh):
    return jax.shard_map(
        on_device,
        mesh=mesh,
        in_specs=(P(("rows", "grp"), None), P(), P(("rows", "grp"))),
        out_specs=(P(("rows", "grp"), None), P(("rows", "grp"), None)),
        check_vma=False,
    )
```

```python
import functools
import math

import jax
import jax.numpy as jnp
from jax import lax
from jax.experimental import pallas as pl
from jax.experimental.pallas import tpu as pltpu
from jax.sharding import PartitionSpec as P

MESH = pl.DeviceIdType.MESH
HIGHEST = lax.Precision.HIGHEST
f32 = jnp.float32
bf16 = jnp.bfloat16

SLOTS = 1024
WIDTH = 4096
COLS = 256
CHIPS = 64
BLOCK = 32
PANEL = 64
GROUP = 16
CHUNKS = 2
VMEM_BYTES = 48 * 1024 * 1024


def dot_t(a, b, precision=None):
    return lax.dot_general(
        a, b, (((0,), (0,)), ((), ())), precision=precision, preferred_element_type=f32
    )


def dot_nt(a, b, precision=None):
    return lax.dot_general(
        a, b, (((1,), (1,)), ((), ())), precision=precision, preferred_element_type=f32
    )


def inverse_of_factor(gram, between=None):
    n = gram.shape[0]
    lane = lax.broadcasted_iota(jnp.int32, (PANEL, n), 1)
    sub = lax.broadcasted_iota(jnp.int32, (PANEL, n), 0)
    sub_narrow = lax.broadcasted_iota(jnp.int32, (PANEL, 128), 0)
    rest = gram
    rows = []
    for start in range(0, n, PANEL):
        end = start + PANEL
        if between is not None and end == n:
            between()
        panel = rest[0:PANEL, :]
        for low in range(0, PANEL, GROUP):
            done, panel = panel[:low], panel[low:]
            left_rows = PANEL - low
            spread = [
                jnp.broadcast_to(panel[:, start + t : start + t + 1], (left_rows, 128))
                for t in range(low, low + GROUP)
            ]
            for k in range(GROUP):
                t = low + k
                j = start + t
                inv = 1.0 / spread[k][k : k + 1, :]
                factor = jnp.where(sub_narrow[:left_rows] > k, spread[k], 0.0)
                for m in range(k + 1, GROUP):
                    spread[m] = spread[m] - factor * (spread[m][k : k + 1, :] * inv)
                pivot = jnp.where(lane[0:1] == j, 1.0, panel[k : k + 1, :])
                pivot = pivot * jnp.concatenate([inv, inv], axis=1)
                below = (sub[:left_rows] > k) & (lane[:left_rows] == j)
                kept = jnp.where(below, 0.0, panel)
                panel = kept - jnp.concatenate([factor, factor], axis=1) * pivot
            panel = panel if low == 0 else jnp.concatenate([done, panel], axis=0)
        diagonal = lane == sub + start
        d = jnp.sum(jnp.where(diagonal, panel, 0.0), axis=1, keepdims=True)
        right = jnp.where(diagonal, 1.0, jnp.where(lane < sub + start, panel, 0.0))
        rows.append(right * lax.rsqrt(d))
        if end < n:
            left = jnp.where(lane >= end, panel, 0.0)
            update = dot_t(left * (1.0 / d), left + right, HIGHEST)
            lane_rest = lax.broadcasted_iota(jnp.int32, (n - end, n), 1)
            inside = (lane_rest >= start) & (lane_rest < end)
            rest = jnp.where(inside, 0.0, rest[PANEL:, :]) - update[end:, :]
    return jnp.concatenate(rows, axis=0)


def range_kernel(
    table_hbm, sketch, counts,
    ortho_out, coeffs_out,
    table, first, rounded, zfull, total,
    zpart, zcore, zsend, zrecv, zblock,
    wpart, wcore, wsend, wrecv,
    gsend, gcore, gsum, grecv, gown, gfull,
    load_sem, core_ss, core_rs, rs_ss, rs_rs, ag_ss, ag_rs, fw_ss, fw_rs,
    g_ss, g_rs, gs_ss, gs_rs, gg_ss, gg_rs, gx_ss, gx_rs,
):
    rows = lax.axis_index("rows")
    x = lax.axis_index("grp")
    core = lax.rem(rows, 2)
    z = lax.rem(rows // 2, 4)
    y = rows // 8
    chip = (y * 4 + z) * 4 + x
    sib = {"rows": rows + 1 - 2 * core}

    def peer(i):
        py = lax.rem(y + i // 16, 4)
        pz = lax.rem(z + lax.rem(i // 4, 4), 4)
        px = lax.rem(x + lax.rem(i, 4), 4)
        return py, pz, px, ((py * 4 + pz) * 2 + core, px)

    def remote(src, dst, ss, rs, device):
        return pltpu.make_async_remote_copy(
            src_ref=src, dst_ref=dst, send_sem=ss, recv_sem=rs,
            device_id=device, device_id_type=MESH,
        )

    def whole(ref, ss, rs):
        return remote(ref, ref, ss, rs, sib)

    loads = []
    for k in range(4):
        r = pl.ds(k * 256, 256)
        loads.append(pltpu.make_async_copy(table_hbm.at[r], table.at[r], load_sem.at[k]))
    for copy in loads:
        copy.start()

    barrier = pltpu.get_barrier_semaphore()

    @pl.loop(1, CHIPS)
    def _(i):
        pl.semaphore_signal(barrier, inc=1, device_id=peer(i)[3], device_id_type=MESH)

    pl.semaphore_signal(barrier, inc=1, device_id=sib, device_id_type=MESH)

    count = counts[0]
    for k in range(4):
        r = pl.ds(k * 256, 256)
        loads[k].wait()
        value = jnp.dot(table[r, :], sketch[...], preferred_element_type=f32)
        used = lax.broadcasted_iota(jnp.int32, (256, COLS), 0) + k * 256 < count
        value = jnp.where(used, value, 0.0)
        first[r, :] = value

    pl.semaphore_wait(barrier, CHIPS)

    zblk = BLOCK // CHUNKS
    sums = [
        (zpart.at[q], zcore.at[q], zsend.at[q], zrecv.at[q], q * (WIDTH // CHUNKS), zblk)
        for q in range(CHUNKS)
    ]
    sums.append((wpart, wcore, wsend, wrecv, 0, BLOCK))

    def line(k, j, sign=1):
        return lax.rem(y + 4 + sign * j, 4) * 4 + lax.rem(z + 4 + sign * ((k - j) % 4), 4)

    def member(i, k):
        j = i // 4
        py = lax.rem(y + j, 4)
        pz = lax.rem(z + lax.rem(k + 4 - j, 4), 4)
        px = lax.rem(x + lax.rem(i, 4), 4)
        return ((py * 4 + pz) * 2 + core, px), px

    def core_copy(q, k):
        part, core_recv = sums[q][:2]
        return remote(
            part.at[k, :, 1 - core], core_recv.at[k], core_ss.at[q, k], core_rs.at[q, k], sib
        )

    def produce(q, k):
        part, _, _, _, base, block = sums[q]
        for j in range(4):
            cols = pl.ds(pl.multiple_of(base + line(k, j) * (8 * block), 8 * block), 8 * block)
            value = dot_t(table[:, cols], rounded[...])
            part[k, j] = value.astype(part.dtype).reshape(2, 4, block, COLS)
        core_copy(q, k).start()

    def spread(q, k):
        part, core_recv, send, recv = sums[q][:4]
        core_copy(q, k).wait_recv()
        mine = part[k, :, core].astype(f32)
        send[k] = (mine + core_recv[k].astype(f32)).astype(send.dtype)

        @pl.loop(1 if k == 0 else 0, 16)
        def _(i):
            device, px = member(i, k)
            remote(
                send.at[k, i // 4, px], recv.at[k * 16 + i], rs_ss.at[q], rs_rs.at[q, k], device
            ).start()

    def reduce_end(q):
        send, recv = sums[q][2:4]
        acc = send[0, 0, x].astype(f32)
        for k in range(4):
            low = k * 16 + (1 if k == 0 else 0)
            n = k * 16 + 16 - low
            whole(recv.at[pl.ds(low, n)], rs_ss.at[q], rs_rs.at[q, k]).wait_recv()
            acc = acc + jnp.sum(recv[pl.ds(low, n)].astype(f32), axis=0)
        return acc

    mine = core * 24
    owner = (chip >= mine) & (chip < mine + 24)

    def gram_exchange(u):
        return remote(
            gsend.at[u, pl.ds(24 - mine, 24)], gcore.at[u], gx_ss.at[u], gx_rs.at[u], sib
        )

    def gram_start(u):
        gram = dot_t(first[...], first[...], HIGHEST)
        gsend[u, pl.ds(0, 16)] = gram[:128, :128].reshape(16, 8, 128)
        gsend[u, pl.ds(16, 16)] = gram[128:, :128].reshape(16, 8, 128)
        gsend[u, pl.ds(32, 16)] = gram[128:, 128:].reshape(16, 8, 128)
        gram_exchange(u).start()

    def gram_send(u):
        gram_exchange(u).wait()
        gsum[u] = gsend[u, pl.ds(mine, 24)] + gcore[u]

        @pl.loop(0, 24)
        def _(k):
            t = mine + k
            device = (((t // 16) * 4 + lax.rem(t // 4, 4)) * 2 + core, lax.rem(t, 4))

            @pl.when(t != chip)
            def _():
                remote(
                    gsum.at[u, k], grecv.at[u, chip], g_ss.at[u], g_rs.at[u], device
                ).start()

    def tiles(u, n, ss, rs):
        return whole(grecv.at[u, pl.ds(0, n)], ss.at[u], rs.at[u])

    def gram_mid(u):
        @pl.when(owner)
        def _():
            grecv[u, chip] = gsum[u, chip - mine]
            tiles(u, 63, g_ss, g_rs).wait_recv()
            tile = jnp.sum(grecv[u], axis=0)
            gown[u] = tile
            gfull[u, chip] = tile

            @pl.loop(1, CHIPS)
            def _(i):
                remote(
                    gown.at[u], gfull.at[u, chip], gg_ss.at[u], gg_rs.at[u], peer(i)[3]
                ).start()

    def gram_end(u):
        @pl.when(owner)
        def _():
            tiles(u, 23, g_ss, gg_rs).wait()
            tiles(u, 63, gg_ss, gg_rs).wait_send()

        @pl.when(jnp.logical_not(owner))
        def _():
            tiles(u, 24, g_ss, gg_rs).wait()

        half = gfull.at[u, pl.ds(mine, 24)]
        back = remote(half, half, gs_ss.at[u], gs_rs.at[u], sib)
        back.start()
        back.wait()
        blocks = [gfull[u, pl.ds(16 * b, 16)].reshape(128, 128) for b in range(3)]
        top = jnp.concatenate([blocks[0], blocks[1].T], axis=1)
        return jnp.concatenate([top, jnp.concatenate(blocks[1:], axis=1)], axis=0)

    def gather_start(q):
        value = reduce_end(q).astype(bf16)
        zblock[q] = value
        home = zfull.at[q, y * 4 + z, core, x]
        home[...] = value
        for k in range(4):

            @pl.loop(1 if k == 0 else 0, 16)
            def _(i):
                device = member(i, k)[0]
                remote(zblock.at[q], home, ag_ss.at[q], ag_rs.at[q, k], device).start()

    def fw_copies(q, k):
        return [
            whole(zfull.at[q, line(k, j, -1), core], fw_ss.at[q, k], fw_rs.at[q, k])
            for j in range(4)
        ]

    def forward(q, k):
        n = 15 if k == 0 else 16
        whole(zfull.at[q, pl.ds(0, n), 0, 0], ag_ss.at[q], ag_rs.at[q, k]).wait_recv()
        for copy in fw_copies(q, k):
            copy.start()

    def multiply(q, k):
        whole(zfull.at[q, pl.ds(0, 4), 0], fw_ss.at[q, k], fw_rs.at[q, k]).wait_recv()
        value = None
        for j in range(4):
            at = line(k, j, -1)
            cols = pl.ds(
                pl.multiple_of(q * (WIDTH // CHUNKS) + at * (8 * zblk), 8 * zblk), 8 * zblk
            )
            piece = zfull[q, at].reshape(8 * zblk, COLS)
            term = jnp.dot(table[:, cols], piece, preferred_element_type=f32)
            value = term if value is None else value + term
        if (q, k) == (0, 0):
            total[...] = value
        else:
            total[...] += value

    steps = [(q, k) for q in range(CHUNKS) for k in range(4)]

    gram_start(0)
    gram_send(0)
    gram_mid(0)
    inverse = inverse_of_factor(gram_end(0))
    rounded[...] = dot_nt(first[...], inverse, HIGHEST).astype(bf16)
    produce(*steps[0])
    for n in range(1, len(steps)):
        produce(*steps[n])
        spread(*steps[n - 1])
    spread(*steps[-1])
    for q in range(CHUNKS):
        gather_start(q)
    forward(*steps[0])
    for n in range(1, len(steps)):
        forward(*steps[n])
        multiply(*steps[n - 1])
    multiply(*steps[-1])

    value = total[...]
    used = lax.broadcasted_iota(jnp.int32, (SLOTS, COLS), 0) < count
    first[...] = jnp.where(used, value, 0.0)
    gram_start(1)

    every = zfull[...].reshape(WIDTH, COLS)
    near = dot_t(every, every)
    gram_send(1)
    near = jnp.dot(near, near, precision=HIGHEST, preferred_element_type=f32)
    guess = inverse_of_factor(near, lambda: gram_mid(1))
    broken = jnp.sum(jnp.where(guess - guess == 0.0, 0.0, 1.0), keepdims=True)
    r = lax.broadcasted_iota(jnp.int32, (COLS, COLS), 0)
    c = lax.broadcasted_iota(jnp.int32, (COLS, COLS), 1)
    guess = jnp.where(broken > 0.0, jnp.where(r == c, 1.0, 0.0), guess)
    value = dot_nt(first[...], guess, HIGHEST)
    first[...] = value
    rounded[...] = value.astype(bf16)

    w = CHUNKS
    produce(w, 0)
    for k in range(1, 4):
        produce(w, k)
        spread(w, k - 1)
    spread(w, 3)

    gram = jnp.dot(guess, gram_end(1), precision=HIGHEST, preferred_element_type=f32)
    inverse = inverse_of_factor(dot_nt(gram, guess, HIGHEST))
    total[...] = dot_nt(first[...], inverse, HIGHEST)
    out = pltpu.make_async_copy(total, ortho_out, load_sem.at[5])
    out.start()
    coeffs_out[...] = dot_nt(reduce_end(w), inverse, HIGHEST)

    out.wait()
    for q in range(CHUNKS + 1):
        for k in range(4):
            core_copy(q, k).wait_send()
        recv = sums[q][3]
        whole(recv.at[pl.ds(1, 63)], rs_ss.at[q], rs_rs.at[q, 0]).wait_send()
    for q in range(CHUNKS):
        for k in range(4):
            n = 15 if k == 0 else 16
            whole(zfull.at[q, pl.ds(0, n), 0, 0], ag_ss.at[q], ag_rs.at[q, k]).wait_send()
            whole(zfull.at[q, pl.ds(0, 4), 0], fw_ss.at[q, k], fw_rs.at[q, k]).wait_send()


def on_device(table, sketch, valid_counts):
    dma = pltpu.SemaphoreType.DMA
    vmem = pltpu.VMEM
    ortho, coeffs = pl.pallas_call(
        range_kernel,
        out_shape=(
            jax.ShapeDtypeStruct((SLOTS, COLS), f32),
            jax.ShapeDtypeStruct((BLOCK, COLS), f32),
        ),
        in_specs=[
            pl.BlockSpec(memory_space=pl.ANY),
            pl.BlockSpec(memory_space=pltpu.VMEM),
            pl.BlockSpec(memory_space=pltpu.SMEM),
        ],
        out_specs=(
            pl.BlockSpec(memory_space=pl.ANY),
            pl.BlockSpec(memory_space=pltpu.VMEM),
        ),
        scratch_shapes=[
            vmem((SLOTS, WIDTH), bf16),
            vmem((SLOTS, COLS), f32),
            vmem((SLOTS, COLS), bf16),
            vmem((CHUNKS, 16, 2, 4, BLOCK // CHUNKS, COLS), bf16),
            vmem((SLOTS, COLS), f32),
            vmem((CHUNKS, 4, 4, 2, 4, BLOCK // CHUNKS, COLS), bf16),
            vmem((CHUNKS, 4, 4, 4, BLOCK // CHUNKS, COLS), bf16),
            vmem((CHUNKS, 4, 4, 4, BLOCK // CHUNKS, COLS), bf16),
            vmem((CHUNKS, CHIPS, BLOCK // CHUNKS, COLS), bf16),
            vmem((CHUNKS, BLOCK // CHUNKS, COLS), bf16),
            vmem((4, 4, 2, 4, BLOCK, COLS), bf16),
            vmem((4, 4, 4, BLOCK, COLS), bf16),
            vmem((4, 4, 4, BLOCK, COLS), bf16),
            vmem((CHIPS, BLOCK, COLS), bf16),
            vmem((2, 48, 8, 128), f32),
            vmem((2, 24, 8, 128), f32),
            vmem((2, 24, 8, 128), f32),
            vmem((2, CHIPS, 8, 128), f32),
            vmem((2, 8, 128), f32),
            vmem((2, 48, 8, 128), f32),
            dma((6,)),
            dma((3, 4)),
            dma((3, 4)),
            dma((3,)),
            dma((3, 4)),
            dma((2,)),
            dma((2, 4)),
            dma((2, 4)),
            dma((2, 4)),
            dma((2,)),
            dma((2,)),
            dma((2,)),
            dma((2,)),
            dma((2,)),
            dma((2,)),
            dma((2,)),
            dma((2,)),
        ],
        compiler_params=pltpu.CompilerParams(
            collective_id=0, has_side_effects=True, vmem_limit_bytes=VMEM_BYTES
        ),
        name="range",
    )(table, sketch, valid_counts)
    return ortho * math.sqrt(SLOTS * 128), coeffs


def solution(mesh):
    return jax.shard_map(
        on_device,
        mesh=mesh,
        in_specs=(P(("rows", "grp"), None), P(), P(("rows", "grp"))),
        out_specs=(P(("rows", "grp"), None), P(("rows", "grp"), None)),
        check_vma=False,
    )
```
